1024 devices in a mesh: grp: 64 (over z, core), loc: 16 (over x, y).
Axes of the slice: x: 4, y: 4, z: 32, core: 2. Of those that a mesh axis runs over, the one named last changes fastest.
Arguments:
- out_grad: bfloat16 [8192, 3584], P('grp', 'loc'), may hold values from -6 to 6
- group_choice: int32 [8192, 4], P('grp'), may hold values from 0 to 63, all different within a row; in each aligned block of 128 rows (0 to 127, 128 to 255, ...) at most 16 rows name the same one
- gate_weight: bfloat16 [8192, 4, 2], P('grp'), may hold values from 0.049804688 to 0.5
- gate_pre: bfloat16 [64, 1024, 2048], P('grp', None, 'loc'), may hold values from -6 to 6
- up_pre: bfloat16 [64, 1024, 2048], P('grp', None, 'loc'), may hold values from -6 to 6
- down_weight: bfloat16 [64, 2048, 3584], P('grp', None, 'loc'), may hold values from -0.1875 to 0.1875
- up_weight: bfloat16 [64, 2048, 3584], P('grp', None, 'loc'), may hold values from -0.1875 to 0.1875
Outputs:
- down_grad: bfloat16 [64, 2048, 3584], P('grp', None, 'loc')
- input_grad: bfloat16 [8192, 3584], P('grp', 'loc')
The draws below stay inside these ranges and needn't reach their ends.
Inputs may be any that keep to these rules, and one draw needn't show every extreme that they name: `group_choice`: A token's 4 groups are distinct. Among the tokens of one index of grp (aligned blocks of 128 tokens) no group is chosen more than 16 times, a bound that some block reaches.
All inputs are finite; a program needn't handle non-finite values. Where the reference program divides by a largest or mean magnitude, that divisor is 1e-20 or more.
Results may differ from the reference program's by a relative error of at most 0.023.
Values may be sent and summed in bfloat16 or wider, within the bound.
A program may use at most 64 MiB of HBM per device.

```python
import math
import jax
import jax.numpy as jnp
import numpy as np
from jax import lax

D = 3584
FF = 1024
EXP_GRP = 2
TOP_GROUPS = 4
TOK_GRP = 128
CAP = 16
SLOTS = 1024
TOKENS = 8192
N_GRP = 64
N_LOC = 16


def steps_of(stream_key, dims, shards, low, high):
    factor_of, own = 1.0, jax.random.fold_in(stream_key, 6)
    for axis_at, shards_of in shards:
        draws = jnp.exp(jax.random.uniform(jax.random.fold_in(own, axis_at), (shards_of,), jnp.float32, low / len(shards), high / len(shards)))
        factor_of = factor_of * jnp.repeat(draws, dims[axis_at] // shards_of).reshape([-1 if axis == axis_at else 1 for axis in range(len(dims))])
    return factor_of


def deal_out(key, own, number, rows, count, top, limit, skew):
    sequence = jax.random.permutation(key, count)
    crowded, usual = portions_of(count, rows * top, limit, skew, True), portions_of(count, rows * top, limit, skew, False)
    places = jnp.arange(count)

    def named(tallies, offset_by):
        used = int((tallies > 0).sum())
        fixed = max(1, used // 4)
        shifted = fixed + (places - fixed + offset_by * (used - fixed)) % max(1, count - fixed)
        return jnp.zeros((count,), jnp.int32).at[sequence[jnp.where(places < fixed, places, shifted)]].set(jnp.asarray(tallies, jnp.int32))

    tallies = jnp.where(number % 4 == 0, named(crowded, number // 4), named(usual, number - number // 4 - 1))
    mixed = jax.random.permutation(jax.random.fold_in(own, 3), count)
    donor, receiver = mixed[0:count // 2 * 2:2], mixed[1:count // 2 * 2:2]
    room = jnp.minimum(tallies[donor] - 1, limit - tallies[receiver]) // 2
    room = jnp.where((donor == sequence[0]) | (receiver == sequence[0]) | (tallies[receiver] == 0), 0, jnp.maximum(room, 0))
    shifted = jax.random.randint(jax.random.fold_in(own, 4), (count // 2,), 0, 1 << 20) % (room + 1)
    tallies = tallies.at[donor].add(-shifted).at[receiver].add(shifted)
    items = jnp.searchsorted(jnp.cumsum(tallies), jnp.arange(rows * top), side="right").astype(jnp.int32)
    table = items.reshape(top, rows).T
    table = table[jax.random.permutation(jax.random.fold_in(own, 1), rows)]
    offset_by = jax.random.randint(jax.random.fold_in(own, 2), (rows, 1), 0, top)
    return jnp.take_along_axis(table, (jnp.arange(top)[None, :] + offset_by) % top, axis=1)


def portions_of(number_of, total, limit, lean, full):
    portions = [(1 << 20) // math.isqrt(grade ** lean) + 1 for grade in range(1, number_of + 1)]
    largest = limit if full else min(limit, max(-(-total // number_of), total * portions[0] // sum(portions)))
    least = 1 if total - largest >= number_of - 1 else 0
    counts, rest = [largest] + [least] * (number_of - 1), total - largest - least * (number_of - 1)
    while rest > 0:
        movable = [i for i in range(1, number_of) if counts[i] < largest] or [i for i in range(1, number_of) if counts[i] < limit]
        whole, remaining = sum([portions[i] for i in movable]), rest
        for i in movable:
            more = min(limit - counts[i], max(1, remaining * portions[i] // whole), rest)
            counts[i] = counts[i] + more
            rest = rest - more
    return np.array(counts)


def noise(rng, extent, width, bound, split=(), kind=jnp.bfloat16):
    result = width * jax.random.normal(rng, extent, jnp.float32)
    if split:
        result = result * steps_of(rng, extent, split, -0.22, 0.18)
    return jnp.clip(result, -bound, bound).astype(kind)


def setup_inputs(seed: int = 0) -> dict:
    key_of = jax.random.split(jax.random.key(seed), 8)
    out_grad = noise(key_of[0], (TOKENS, D), 1.0, 6.0, ((0, 64), (1, 16)))
    group_choice_keys = jax.random.split(jax.random.fold_in(key_of[1], 1), TOKENS // TOK_GRP)
    group_choice_turns = jax.random.permutation(jax.random.fold_in(key_of[1], 3), TOKENS // TOK_GRP)
    group_choice = jax.vmap(lambda own, number: deal_out(jax.random.fold_in(key_of[1], 2), own, number, TOK_GRP, N_GRP, TOP_GROUPS, CAP, 2))(group_choice_keys, group_choice_turns).reshape((TOKENS, TOP_GROUPS))
    gate_weight = jnp.clip(jnp.exp(math.log(0.5) - 2.306499 * jax.random.uniform(key_of[2], (TOKENS, TOP_GROUPS, EXP_GRP), jnp.float32) ** steps_of(key_of[2], (TOKENS, TOP_GROUPS, EXP_GRP), ((0, 64),), -0.2, 0.2)), 0.049804688, 0.5).astype(jnp.bfloat16)
    gate_pre = noise(key_of[3], (N_GRP, SLOTS, EXP_GRP * FF), 1.5, 6.0, ((0, 64), (2, 16)))
    up_pre = noise(key_of[4], (N_GRP, SLOTS, EXP_GRP * FF), 1.0, 6.0, ((0, 64), (2, 16)))
    down_weight = noise(key_of[5], (N_GRP, EXP_GRP * FF, D), FF ** -0.5, 0.1875, ((0, 64), (2, 16)))
    up_weight = noise(key_of[6], (N_GRP, EXP_GRP * FF, D), FF ** -0.5, 0.1875, ((0, 64), (2, 16)))
    return {"out_grad": out_grad, "group_choice": group_choice, "gate_weight": gate_weight, "gate_pre": gate_pre, "up_pre": up_pre, "down_weight": down_weight, "up_weight": up_weight}


def routing(group_choice):
    blocks = group_choice.reshape(N_GRP, TOK_GRP, TOP_GROUPS)
    picked = (blocks[:, :, :, None] == jnp.arange(N_GRP, dtype=jnp.int32)[None, None, None, :]).astype(jnp.int32)
    group_load = jnp.sum(picked, axis=2)
    earlier = jnp.cumsum(group_load, axis=1) - group_load
    position = jnp.sum(picked * earlier[:, :, None, :], axis=3)
    source = jnp.arange(N_GRP, dtype=jnp.int32)[:, None, None]
    flat_slot = blocks * SLOTS + source * CAP + position
    return flat_slot.reshape(TOKENS, TOP_GROUPS).astype(jnp.int32)


def per_group(inputs):
    slot_rows, slot_gate, gate_pre, up_pre, down_weight, up_weight = inputs
    block_width = D // N_LOC
    weighted = slot_gate.astype(jnp.float32)[:, :, None] * slot_rows.astype(jnp.float32)[:, None, :]
    weighted_bf = weighted.astype(jnp.bfloat16)
    left = weighted_bf.reshape(SLOTS, EXP_GRP, N_LOC, block_width).astype(jnp.float32)
    right = down_weight.reshape(EXP_GRP, FF, N_LOC, block_width).astype(jnp.float32)
    partial_value = jnp.einsum("renk,efnk->nref", left, right).astype(jnp.bfloat16)
    partial_value = lax.optimization_barrier(partial_value)
    hidden_grad = jnp.sum(partial_value.astype(jnp.float32), axis=0).reshape(SLOTS, EXP_GRP * FF)
    activation = jax.nn.silu(gate_pre.astype(jnp.float32))
    hidden = (activation * up_pre.astype(jnp.float32)).astype(jnp.bfloat16)
    up_grad = (hidden_grad * activation).astype(jnp.bfloat16)
    column_scale = jnp.max(jnp.abs(weighted), axis=0) + 1e-6
    quantized = (weighted / column_scale[None, :, :]).astype(jnp.bfloat16)
    weight_grad = jnp.einsum("ref,red->efd", hidden.reshape(SLOTS, EXP_GRP, FF).astype(jnp.float32), quantized.astype(jnp.float32))
    weight_grad = (weight_grad * column_scale[:, None, :]).astype(jnp.bfloat16).reshape(EXP_GRP * FF, D)
    returning = jnp.dot(up_grad, up_weight, preferred_element_type=jnp.float32).astype(jnp.bfloat16)
    return weight_grad, returning


def reference(out_grad, group_choice, gate_weight, gate_pre, up_pre, down_weight, up_weight):
    flat_slot = routing(group_choice).reshape(-1)
    total_rows = N_GRP * SLOTS
    slot_rows = jnp.zeros((total_rows, D), jnp.bfloat16).at[flat_slot].set(jnp.repeat(out_grad, TOP_GROUPS, axis=0))
    slot_gate = jnp.zeros((total_rows, EXP_GRP), jnp.bfloat16).at[flat_slot].set(gate_weight.reshape(TOKENS * TOP_GROUPS, EXP_GRP))
    down_grad, returning = lax.map(per_group, (slot_rows.reshape(N_GRP, SLOTS, D), slot_gate.reshape(N_GRP, SLOTS, EXP_GRP), gate_pre, up_pre, down_weight, up_weight))
    picked_rows = returning.reshape(total_rows, D)[flat_slot].astype(jnp.float32).reshape(TOKENS, TOP_GROUPS, D)
    input_grad = jnp.sum(picked_rows, axis=1).astype(jnp.bfloat16)
    return down_grad, input_grad
```

```python
import functools

import jax
import jax.numpy as jnp
from jax import lax
from jax.experimental import pallas as pl
from jax.experimental.pallas import tpu as pltpu
from jax.sharding import PartitionSpec as P

MESH = pl.DeviceIdType.MESH
NT = (((1,), (1,)), ((), ()))
TN = (((0,), (0,)), ((), ()))
F32 = jnp.float32
BF16 = jnp.bfloat16
ZP = 3
RP = 2


def moe_kernel(
    x_ref, choice_ref, gates_ref, gp_ref, up_ref, wd_ref, wu_ref,
    dg_ref, ig_ref,
    allx, wf, wbf, wt, qt, cst, act, gh0, gh1, gu0, gu1, pa0, pa1, op0, op1, ma0, ma1,
    s10, s11, op20, op21, ma20, ma21, ret, own, sibs, sibr, ringr, rings,
    zsend, zrecv, bsend, brecv, xsend, xrecv, rsend, rrecv, csend, crecv,
):
    n_grp = allx.shape[0]
    n_z = n_grp // 2
    half = n_z // 2
    feats, toks = x_ref.shape
    meta_rows = allx.shape[1] - feats
    slots = gp_ref.shape[0]
    cap = slots // n_grp
    hw = gp_ref.shape[1]
    hs = slots // 2
    qs = hs // 2
    picks = choice_ref.shape[0]
    per_e = 8

    g = lax.axis_index("grp")
    loc = lax.axis_index("loc")
    z, c = lax.div(g, 2), lax.rem(g, 2)
    x, y = lax.div(loc, 4), lax.rem(loc, 4)
    gz = lambda r: lax.rem(z + r + 2 * n_z, n_z)
    zdev = [(gz(1) * 2 + c, loc), (gz(-1) * 2 + c, loc)]
    sib = (z * 2 + 1 - c, loc)
    xdev = [(g, lax.rem(x + 1, 4) * 4 + y), (g, lax.rem(x + 3, 4) * 4 + y)]
    ydev = [(g, x * 4 + lax.rem(y + 1, 4)), (g, x * 4 + lax.rem(y + 3, 4))]
    pos1, pos2 = [x, y], [y, x]
    dev1, dev2 = [xdev, ydev], [ydev, xdev]
    gh, gu, part = [gh0, gh1], [gu0, gu1], [pa0, pa1]
    opp, main = [op0, op1], [ma0, ma1]
    s1, opp2, main2 = [s10, s11], [op20, op21], [ma20, ma21]

    def copy(src, dst, ss, rs, dev):
        return pltpu.make_async_remote_copy(
            src_ref=src, dst_ref=dst, send_sem=ss, recv_sem=rs, device_id=dev, device_id_type=MESH
        )

    barrier = pltpu.get_barrier_semaphore()
    for dev in zdev + [sib] + xdev + ydev:
        pl.semaphore_signal(barrier, inc=1, device_id=dev, device_id_type=MESH)

    choice = choice_ref[...].astype(F32)
    ids = lax.broadcasted_iota(jnp.int32, (n_grp, toks), 0).astype(F32)
    hits = [choice[k : k + 1] == ids for k in range(picks)]
    load = sum(h.astype(F32) for h in hits).astype(BF16)
    before = (
        lax.broadcasted_iota(jnp.int32, (toks, toks), 0) < lax.broadcasted_iota(jnp.int32, (toks, toks), 1)
    ).astype(F32).astype(BF16)
    earlier = jnp.dot(load, before, preferred_element_type=F32)
    row8 = lax.broadcasted_iota(jnp.int32, (8, toks), 0)
    low = jnp.zeros((8, toks), F32)
    for k in range(picks):
        place = jnp.sum(jnp.where(hits[k], earlier, 0.0), axis=0, keepdims=True)
        low = jnp.where(row8 == k, choice[k : k + 1], low)
        low = jnp.where(row8 == picks + k, place, low)
    meta = jnp.concatenate([gates_ref[...].astype(F32), low], axis=0)
    allx[g, 0:feats, :] = x_ref[...]
    allx[g, feats:, :] = meta.astype(BF16)

    pl.semaphore_wait(barrier, 7)

    zrows = allx.shape[1] // ZP

    def blk(r):
        return gz(r) * 2 + c

    def zcopy(d, s, p):
        ref = allx.at[blk(-s if d == 0 else s), pl.ds(p * zrows, zrows), :]
        return copy(ref, ref, zsend.at[d, s, p], zrecv.at[d, s, p], zdev[d])

    def zwait(d, s, p):
        ref = allx.at[blk(-(s + 1) if d == 0 else s + 1), pl.ds(p * zrows, zrows), :]
        copy(ref, ref, zsend.at[d, s, p], zrecv.at[d, s, p], zdev[d]).wait_recv()

    def bcopy(d, s):
        ref = allx.at[blk(-s if d == 0 else s)]
        return copy(ref, ref, bsend.at[d, s], brecv.at[d, s], sib)

    def bwait(d, s):
        ref = allx.at[gz(-s if d == 0 else s) * 2 + 1 - c]
        copy(ref, ref, bsend.at[d, s], brecv.at[d, s], sib).wait_recv()

    gf = g.astype(F32)

    def chosen(i):
        m = allx[i, feats:, :].astype(F32)
        place = jnp.full((1, toks), -1.0, F32)
        gate = [jnp.zeros((1, toks), F32), jnp.zeros((1, toks), F32)]
        for k in range(picks):
            sel = m[8 + k : 9 + k] == gf
            place = jnp.where(sel, m[8 + picks + k : 9 + picks + k], place)
            for e in range(2):
                gate[e] = jnp.where(sel, m[2 * k + e : 2 * k + e + 1], gate[e])
        hit = lax.broadcasted_iota(jnp.int32, (cap, toks), 0).astype(F32) == place
        return hit, gate

    def build(i):
        hit, gate = chosen(i)
        lhs = jnp.concatenate([jnp.where(hit, gate[0], 0.0), jnp.where(hit, gate[1], 0.0)], axis=0).astype(BF16)
        w = lax.dot_general(lhs, allx[i, 0:feats, :], NT, preferred_element_type=F32)
        at = pl.ds(pl.multiple_of(i * cap, cap), cap)
        for e in range(2):
            wf[e, at, 0:feats] = w[e * cap : (e + 1) * cap]
            wbf[e, at, 0:feats] = w[e * cap : (e + 1) * cap].astype(BF16)

    def zstep(s, up=True, down=True, lag=True):
        for p in range(ZP):
            zwait(0, s - 1, p)
            if up:
                zcopy(0, s, p).start()
            if down is not None:
                zwait(1, s - 1, p)
                if down:
                    zcopy(1, s, p).start()
        bcopy(0, s).start()
        build(blk(-s))
        if down is not None:
            bcopy(1, s).start()
            build(blk(s))
        if lag:
            for d in range(2):
                bwait(d, s - 1)
                build(gz(-(s - 1) if d == 0 else s - 1) * 2 + 1 - c)

    def zloop(lo, hi):
        lo, hi = min(lo, half - 1), min(hi, half - 1)
        if lo < hi:
            def step(s, carry):
                zstep(s)
                return carry
            lax.fori_loop(lo, hi, step, 0)

    def ring(stage, h):
        a = (pos1 if stage in (0, 3, 5) else pos2)[h]
        dev = (dev1 if stage in (0, 3, 5) else dev2)[h]
        nxt = [lax.rem(a + 1, 4), lax.rem(a + 3, 4)]
        return a, dev, nxt, lax.rem(a + 2, 4)

    def xcopy(stage, h, side, n, src, dst):
        _, dev, _, _ = ring(stage, h)
        return copy(src, dst, xsend.at[stage, h, side, n], xrecv.at[stage, h, side, n], dev[side])

    def rs_refs(stage, h):
        return (part[h], opp[h], main[h]) if stage == 0 else (s1[h], opp2[h], main2[h])

    def rs_copy(stage, h, side, n):
        _, _, nxt, far = ring(stage, h)
        src, o, m = rs_refs(stage, h)
        if n == 0:
            return xcopy(stage, h, side, 0, src.at[far, side], o.at[side])
        if n == 1:
            return xcopy(stage, h, side, 1, src.at[nxt[side], 1 - side], m.at[side, 1 - side])
        return xcopy(stage, h, side, 2, src.at[nxt[side], side], m.at[side, side])

    def rs_add(stage, h, side):
        _, _, nxt, _ = ring(stage, h)
        src, o, _ = rs_refs(stage, h)
        rs_copy(stage, h, side, 0).wait_recv()
        rows = src.shape[2]
        piece = min(rows, 128)

        def step(q, carry):
            at = pl.ds(pl.multiple_of(q * piece, piece), piece)
            total = src[nxt[side], side, at, :].astype(F32) + o[side, at, :].astype(F32)
            src[nxt[side], side, at, :] = total.astype(BF16)
            return carry

        lax.fori_loop(0, rows // piece, step, 0)
        rs_copy(stage, h, side, 2).start()

    def rs_wait_main(stage, h):
        for side in range(2):
            rs_copy(stage, h, side, 1).wait_recv()
            rs_copy(stage, h, side, 2).wait_recv()

    def ag_ref(stage, store, h, who, k):
        if stage in (3, 5):
            return store[h].at[who, k]
        a = pos1[h]
        return store[h].at[a, lax.div(who, 2), pl.ds(pl.multiple_of(lax.rem(who, 2) * hs + k * qs, qs), qs), :]

    def ag_copy(stage, store, h, side, n):
        a, _, nxt, _ = ring(stage, h)
        if n == 2:
            ref = ag_ref(stage, store, h, nxt[1 - side], side)
        else:
            ref = ag_ref(stage, store, h, a, side if n == 0 else 1 - side)
        return xcopy(stage, h, side, n, ref, ref)

    def ag_wait(stage, store, h, side, n):
        _, _, nxt, far = ring(stage, h)
        if n == 2:
            ref = ag_ref(stage, store, h, far, side)
        else:
            ref = ag_ref(stage, store, h, nxt[1 - side], side if n == 0 else 1 - side)
        xcopy(stage, h, side, n, ref, ref).wait_recv()

    def ag_send(stage, store, h):
        for n in range(2):
            for side in range(2):
                ag_copy(stage, store, h, side, n).start()

    def ag_pass(stage, store, h):
        for side in range(2):
            ag_wait(stage, store, h, side, 0)
            ag_copy(stage, store, h, side, 2).start()

    def ag_finish(stage, store, h):
        for side in range(2):
            ag_wait(stage, store, h, side, 1)
            ag_wait(stage, store, h, side, 2)

    def own_rows(h, k):
        return (pos1[h], lax.div(pos2[h], 2), pl.ds(pl.multiple_of(lax.rem(pos2[h], 2) * hs + k * qs, qs), qs))

    for p in range(ZP):
        for d in range(2):
            zcopy(d, 0, p).start()
    bcopy(0, 0).start()

    for h in range(2):
        for k in range(2):
            at = pl.ds(h * hs + k * qs, qs)
            v = gp_ref[at, :].astype(F32)
            a = v / (1.0 + jnp.exp(-v))
            act[at, :] = a
            i0, i1, i2 = own_rows(h, k)
            gh[h][i0, i1, i2, :] = (a * up_ref[at, :].astype(F32)).astype(BF16)
    for h in range(2):
        ag_send(2, gh, h)
    build(g)
    bwait(0, 0)
    build(z * 2 + 1 - c)

    zstep(1, down=half > 2, lag=False)
    zloop(2, 4)
    for h in range(2):
        ag_pass(2, gh, h)
    zloop(4, 6)
    for h in range(2):
        ag_finish(2, gh, h)
        ag_send(3, gh, h)
    zloop(6, 12)
    for h in range(2):
        ag_pass(3, gh, h)
    zloop(12, half - 1)
    if half > 2:
        zstep(half - 1, down=False)
    zstep(half, up=False, down=None)
    bwait(0, half)
    build(gz(-half) * 2 + 1 - c)

    def partial(h, t):
        def step(q, carry):
            b = lax.div(q, 2)
            l = t * 4 + b if h == 0 else b * 4 + t
            rows = pl.ds(pl.multiple_of(h * hs + lax.rem(q, 2) * qs, qs), qs)
            v = jnp.dot(
                wbf[lax.div(l, per_e), rows, 0:feats],
                wd_ref[:, pl.ds(pl.multiple_of(l * hw, hw), hw)],
                preferred_element_type=F32,
            )
            part[h][t, lax.div(q, 4), pl.ds(pl.multiple_of(lax.rem(q, 4) * qs, qs), qs), :] = v.astype(BF16)
            return carry

        lax.fori_loop(0, 8, step, 0)

    for h in range(2):
        partial(h, ring(0, h)[3])
        for side in range(2):
            rs_copy(0, h, side, 0).start()
    for side in range(2):
        for h in range(2):
            partial(h, ring(0, h)[2][side])
            rs_copy(0, h, side, 1).start()
    for h in range(2):
        for side in range(2):
            rs_add(0, h, side)
    for h in range(2):
        partial(h, ring(0, h)[0])

    def turn(q, carry):
        at = pl.ds(pl.multiple_of(q * 128, 128), 128)
        for e in range(2):
            for k in range(0, wf.shape[2], 128):
                wt[e, k : k + 128, at] = wf[e, at, k : k + 128].T
        return carry

    lax.fori_loop(0, slots // 128, turn, 0)
    for e in range(2):
        top = jnp.max(jnp.abs(wt[e, 0:feats, :]), axis=1, keepdims=True) + 1e-6
        cst[e] = jnp.broadcast_to(top, (feats, 128))

    def scale(q, carry):
        at = pl.ds(pl.multiple_of(q * 128, 128), 128)
        for e in range(2):
            qt[e, :, at] = (wt[e, 0:feats, at] / cst[e]).astype(BF16)
        return carry

    lax.fori_loop(0, slots // 128, scale, 0)

    for h in range(2):
        rs_wait_main(0, h)

        def add1(q, carry):
            k = lax.div(q, 4)
            at = pl.ds(pl.multiple_of(lax.rem(q, 4) * qs, qs), qs)
            total = (
                part[h][pos1[h], k, at, :].astype(F32)
                + main[h][0, k, at, :].astype(F32)
                + main[h][1, k, at, :].astype(F32)
            )
            s1[h][lax.div(q, 2), lax.rem(q, 2)] = total.astype(BF16)
            return carry

        lax.fori_loop(0, 8, add1, 0)
        for side in range(2):
            rs_copy(1, h, side, 0).start()
            rs_copy(1, h, side, 1).start()
    for h in range(2):
        for side in range(2):
            rs_add(1, h, side)
    for h in range(2):
        ag_finish(3, gh, h)
    for h in range(2):
        rs_wait_main(1, h)
        for k in range(2):
            at = pl.ds(h * hs + k * qs, qs)
            total = (
                s1[h][pos2[h], k].astype(F32) + main2[h][0, k].astype(F32) + main2[h][1, k].astype(F32)
            )
            i0, i1, i2 = own_rows(h, k)
            gu[h][i0, i1, i2, :] = (total * act[at, :]).astype(BF16)
        ag_send(4, gu, h)
    for h in range(2):
        ag_pass(4, gu, h)
    for h in range(2):
        ag_finish(4, gu, h)
        ag_send(5, gu, h)

    def grad(q, carry):
        e = lax.div(q, per_e)
        xx, yy = lax.div(q, 4), lax.rem(q, 4)
        at = pl.ds(pl.multiple_of(q * hw, hw), hw)
        total = jnp.zeros((feats, hw), F32)
        for h, (i, j) in enumerate(((xx, yy), (yy, xx))):
            hid = gh[h][i, lax.div(j, 2), pl.ds(pl.multiple_of(lax.rem(j, 2) * hs, hs), hs), :]
            total += jnp.dot(qt[e, :, h * hs : (h + 1) * hs], hid, preferred_element_type=F32)
        dg_ref[:, at] = (total * cst[e]).astype(BF16)
        return carry

    lax.fori_loop(0, 8, grad, 0)
    for h in range(2):
        ag_pass(5, gu, h)
    lax.fori_loop(8, 16, grad, 0)
    for h in range(2):
        ag_finish(5, gu, h)

        def back(q, carry):
            total = jnp.zeros((qs, feats), F32)
            for i in range(4):
                for j in range(4):
                    l = i * 4 + j if h == 0 else j * 4 + i
                    up = gu[h][i, j // 2, pl.ds(pl.multiple_of((j % 2) * hs + q * qs, qs), qs), :]
                    total += lax.dot_general(up, wu_ref[:, l * hw : (l + 1) * hw], NT, preferred_element_type=F32)
            ret[pl.ds(pl.multiple_of(h * hs + q * qs, qs), qs), 0:feats] = total.astype(BF16)
            return carry

        lax.fori_loop(0, 2, back, 0)

    rrows = feats // RP

    def contrib(n):
        zt = gz(n)
        i, j = zt * 2 + c, zt * 2 + 1 - c
        rows = jnp.concatenate(
            [
                ret[pl.ds(pl.multiple_of(i * cap, cap), cap), 0:feats],
                ret[pl.ds(pl.multiple_of(j * cap, cap), cap), 0:feats],
            ],
            axis=0,
        )
        mine, other = chosen(i)[0].astype(F32), chosen(j)[0].astype(F32)
        none = jnp.zeros((cap, toks), F32)
        pick = jnp.concatenate(
            [jnp.concatenate([mine, none], axis=1), jnp.concatenate([none, other], axis=1)], axis=0
        ).astype(BF16)
        v = lax.dot_general(rows, pick, TN, preferred_element_type=F32).astype(BF16)
        own[n] = v[:, 0:toks]
        sibs[n] = v[:, toks:]
        copy(sibs.at[n], sibr.at[n], csend.at[n], crecv.at[n], sib).start()

    def cwait(n):
        copy(sibs.at[n], sibr.at[n], csend.at[n], crecv.at[n], sib).wait_recv()

    def index(d, s):
        return half - s if d == 0 else lax.rem(half + 1 + s, n_z)

    def rcopy(d, s, p):
        at = pl.ds(p * rrows, rrows)
        return copy(rings.at[d, s, at, :], ringr.at[d, s, at, :], rsend.at[d, s, p], rrecv.at[d, s, p], zdev[d])

    def rstep(s, first=False, both=True):
        dirs = (0, 1) if both else (0,)
        for d in dirs:
            cwait(index(d, s))
        for p in range(RP):
            at = slice(p * rrows, (p + 1) * rrows)
            for d in dirs:
                n = index(d, s)
                total = own[n, at, :].astype(F32) + sibr[n, at, :].astype(F32)
                if not first:
                    rcopy(d, s - 1, p).wait_recv()
                    total += ringr[d, s - 1, at, :].astype(F32)
                rings[d, s, at, :] = total.astype(BF16)
                rcopy(d, s, p).start()

    contrib(index(0, 0))
    contrib(index(1, 0))
    contrib(index(0, 1))
    contrib(index(1, 1))
    rstep(0, first=True)

    def rloop(s, carry):
        contrib(index(0, s + 1))
        contrib(index(1, s + 1))
        rstep(s)
        return carry

    lax.fori_loop(1, half - 1, rloop, 0)
    rstep(half - 1, both=False)
    cwait(0)
    for p in range(RP):
        at = slice(p * rrows, (p + 1) * rrows)
        rcopy(0, half - 1, p).wait_recv()
        rcopy(1, half - 2, p).wait_recv()
        ig_ref[at, :] = (
            own[0, at, :].astype(F32)
            + sibr[0, at, :].astype(F32)
            + ringr[0, half - 1, at, :].astype(F32)
            + ringr[1, half - 2, at, :].astype(F32)
        ).astype(BF16)

    def drain(lo, hi, what):
        def step(s, carry):
            what(s)
            return carry
        lax.fori_loop(lo, hi, step, 0)

    for d in range(2):
        for p in range(ZP):
            drain(0, half - d, lambda s: zcopy(d, s, p).wait_send())
        for p in range(RP):
            drain(0, half - d, lambda s: rcopy(d, s, p).wait_send())
    drain(0, half + 1, lambda s: bcopy(0, s).wait_send())
    drain(1, half, lambda s: bcopy(1, s).wait_send())
    drain(0, n_z, lambda n: copy(sibs.at[n], sibr.at[n], csend.at[n], crecv.at[n], sib).wait_send())
    for h in range(2):
        for side in range(2):
            for n in range(3):
                for stage in (0, 1):
                    rs_copy(stage, h, side, n).wait_send()
                for stage, store in ((2, gh), (3, gh), (4, gu), (5, gu)):
                    ag_copy(stage, store, h, side, n).wait_send()


def on_device(out_grad, group_choice, gate_weight, gate_pre, up_pre, down_weight, up_weight):
    n_grp = lax.axis_size("grp")
    half = n_grp // 4
    toks, feats = out_grad.shape
    picks, experts = gate_weight.shape[1:]
    slots, hw = gate_pre.shape[1:]
    hidden = down_weight.shape[1]
    hs, qs = slots // 2, slots // 4
    wide = -(-feats // 128) * 128
    vm = lambda shape, kind=BF16: pltpu.VMEM(shape, kind)
    sem = lambda *shape: pltpu.SemaphoreType.DMA(shape)
    meta = picks * (experts + 2)
    scratch = [
        vm((n_grp, feats + meta, toks)),
        vm((experts, slots, wide), F32), vm((experts, slots, wide)),
        vm((experts, wide, slots), F32), vm((experts, feats, slots)), vm((experts, feats, 128), F32),
        vm((slots, hw), F32),
        *[vm((4, 2, 2 * hs, hw)) for _ in range(6)],
        *[vm((2, 2 * hs, hw)) for _ in range(2)],
        *[vm((2, 2, 2 * hs, hw)) for _ in range(2)],
        *[vm((4, 2, qs, hw)) for _ in range(2)],
        *[vm((2, qs, hw)) for _ in range(2)],
        *[vm((2, 2, qs, hw)) for _ in range(2)],
        vm((slots, wide)),
        *[vm((n_grp // 2, feats, toks)) for _ in range(3)],
        *[vm((2, half, feats, toks)) for _ in range(2)],
        sem(2, half, ZP), sem(2, half, ZP), sem(2, half + 1), sem(2, half + 1),
        sem(6, 2, 2, 3), sem(6, 2, 2, 3),
        sem(2, half, RP), sem(2, half, RP), sem(n_grp // 2), sem(n_grp // 2),
    ]
    whole = pl.BlockSpec(memory_space=pltpu.VMEM)
    down_t, input_t = pl.pallas_call(
        moe_kernel,
        out_shape=(
            jax.ShapeDtypeStruct((feats, hidden), BF16),
            jax.ShapeDtypeStruct((feats, toks), BF16),
        ),
        in_specs=[whole] * 7,
        out_specs=(whole, whole),
        scratch_shapes=scratch,
        compiler_params=pltpu.CompilerParams(
            collective_id=0, has_side_effects=True, vmem_limit_bytes=58 * 1024 * 1024
        ),
    )(
        out_grad.T,
        group_choice.T,
        gate_weight.transpose(1, 2, 0).reshape(picks * experts, toks),
        gate_pre[0],
        up_pre[0],
        down_weight[0].T,
        up_weight[0].T,
    )
    return down_t.T[None], input_t.T


def solution(mesh):
    return jax.shard_map(
        on_device,
        mesh=mesh,
        in_specs=(
            P("grp", "loc"),
            P("grp", None),
            P("grp", None, None),
            P("grp", None, "loc"),
            P("grp", None, "loc"),
            P("grp", None, "loc"),
            P("grp", None, "loc"),
        ),
        out_specs=(P("grp", None, "loc"), P("grp", "loc")),
        check_vma=False,
    )
```

```python
import functools

import jax
import jax.numpy as jnp
from jax import lax
from jax.experimental import pallas as pl
from jax.experimental.pallas import tpu as pltpu
from jax.sharding import PartitionSpec as P

MESH = pl.DeviceIdType.MESH
NT = (((1,), (1,)), ((), ()))
TN = (((0,), (0,)), ((), ()))
F32 = jnp.float32
BF16 = jnp.bfloat16
JUMP = 2
OUT = 3
BACK = 2


def moe_kernel(
    x_ref, choice_ref, gates_ref, gp_ref, up_ref, wd_ref, wu_ref,
    dg_ref, ig_ref,
    allx, wf, wbf, wt, qt, cst, act, gh0, gh1, gu0, gu1, pa0, pa1, op0, op1, ma0, ma1,
    s10, s11, op20, op21, ma20, ma21, ret, own, sibs, sibr, ringr, rings,
    zsend, zrecv, bsend, brecv, xsend, xrecv, rsend, rrecv, csend, crecv,
):
    n_grp = allx.shape[0]
    n_z = n_grp // 2
    half = n_z // 2
    feats, toks = x_ref.shape
    meta_rows = allx.shape[1] - feats
    slots = gp_ref.shape[0]
    cap = slots // n_grp
    hw = gp_ref.shape[1]
    hs = slots // 2
    qs = hs // 2
    picks = choice_ref.shape[0]
    per_e = 8

    g = lax.axis_index("grp")
    loc = lax.axis_index("loc")
    z, c = lax.div(g, 2), lax.rem(g, 2)
    x, y = lax.div(loc, 4), lax.rem(loc, 4)
    gz = lambda r: lax.rem(z + r + 2 * n_z, n_z)
    zdev = [(gz(1) * 2 + c, loc), (gz(-1) * 2 + c, loc)]
    sib = (z * 2 + 1 - c, loc)
    xdev = [(g, lax.rem(x + 1, 4) * 4 + y), (g, lax.rem(x + 3, 4) * 4 + y)]
    ydev = [(g, x * 4 + lax.rem(y + 1, 4)), (g, x * 4 + lax.rem(y + 3, 4))]
    pos1, pos2 = [x, y], [y, x]
    dev1, dev2 = [xdev, ydev], [ydev, xdev]
    gh, gu, part = [gh0, gh1], [gu0, gu1], [pa0, pa1]
    opp, main = [op0, op1], [ma0, ma1]
    s1, opp2, main2 = [s10, s11], [op20, op21], [ma20, ma21]

    def copy(src, dst, ss, rs, dev):
        return pltpu.make_async_remote_copy(
            src_ref=src, dst_ref=dst, send_sem=ss, recv_sem=rs, device_id=dev, device_id_type=MESH
        )

    barrier = pltpu.get_barrier_semaphore()
    far = [(gz(r) * 2 + c, loc) for j in range(2, JUMP + 1) for r in (j, -j)]
    greeted = zdev + far + [sib] + xdev + ydev
    for dev in greeted:
        pl.semaphore_signal(barrier, inc=1, device_id=dev, device_id_type=MESH)

    choice = choice_ref[...].astype(F32)
    ids = lax.broadcasted_iota(jnp.int32, (n_grp, toks), 0).astype(F32)
    hits = [choice[k : k + 1] == ids for k in range(picks)]
    load = sum(h.astype(F32) for h in hits).astype(BF16)
    before = (
        lax.broadcasted_iota(jnp.int32, (toks, toks), 0) < lax.broadcasted_iota(jnp.int32, (toks, toks), 1)
    ).astype(F32).astype(BF16)
    earlier = jnp.dot(load, before, preferred_element_type=F32)
    row8 = lax.broadcasted_iota(jnp.int32, (8, toks), 0)
    low = jnp.zeros((8, toks), F32)
    for k in range(picks):
        place = jnp.sum(jnp.where(hits[k], earlier, 0.0), axis=0, keepdims=True)
        low = jnp.where(row8 == k, choice[k : k + 1], low)
        low = jnp.where(row8 == picks + k, place, low)
    meta = jnp.concatenate([gates_ref[...].astype(F32), low], axis=0)
    allx[g, 0:feats, :] = x_ref[...]
    allx[g, feats:, :] = meta.astype(BF16)

    pl.semaphore_wait(barrier, len(greeted))


    def blk(r):
        return gz(r) * 2 + c

    def base(d):
        return (d - 1) // JUMP * JUMP if isinstance(d, int) else lax.div(d - 1, JUMP) * JUMP

    zrows = allx.shape[1] // OUT

    def zcopy(w, d, p):
        b = base(d)
        ref = allx.at[blk(-b if w == 0 else b), pl.ds(p * zrows, zrows), :]
        dev = (blk(d - b if w == 0 else b - d), loc)
        return copy(ref, ref, zsend.at[w, d - 1, p], zrecv.at[w, d - 1, p], dev)

    def zwait(w, d, p):
        ref = allx.at[blk(-d if w == 0 else d), pl.ds(p * zrows, zrows), :]
        copy(ref, ref, zsend.at[w, d - 1, p], zrecv.at[w, d - 1, p], zdev[w]).wait_recv()

    def bcopy(d, s):
        ref = allx.at[blk(-s if d == 0 else s)]
        return copy(ref, ref, bsend.at[d, s], brecv.at[d, s], sib)

    def bwait(d, s):
        ref = allx.at[gz(-s if d == 0 else s) * 2 + 1 - c]
        copy(ref, ref, bsend.at[d, s], brecv.at[d, s], sib).wait_recv()

    gf = g.astype(F32)

    def chosen(i):
        m = allx[i, feats:, :].astype(F32)
        place = jnp.full((1, toks), -1.0, F32)
        gate = [jnp.zeros((1, toks), F32), jnp.zeros((1, toks), F32)]
        for k in range(picks):
            sel = m[8 + k : 9 + k] == gf
            place = jnp.where(sel, m[8 + picks + k : 9 + picks + k], place)
            for e in range(2):
                gate[e] = jnp.where(sel, m[2 * k + e : 2 * k + e + 1], gate[e])
        hit = lax.broadcasted_iota(jnp.int32, (cap, toks), 0).astype(F32) == place
        return hit, gate

    def build(i):
        hit, gate = chosen(i)
        lhs = jnp.concatenate([jnp.where(hit, gate[0], 0.0), jnp.where(hit, gate[1], 0.0)], axis=0).astype(BF16)
        w = lax.dot_general(lhs, allx[i, 0:feats, :], NT, preferred_element_type=F32)
        at = pl.ds(pl.multiple_of(i * cap, cap), cap)
        for e in range(2):
            wf[e, at, 0:feats] = w[e * cap : (e + 1) * cap]
            wbf[e, at, 0:feats] = w[e * cap : (e + 1) * cap].astype(BF16)

    def zpass(k):
        for p in range(OUT):
            for w in range(2):
                if 0 < k * JUMP <= half - w:
                    zwait(w, k * JUMP, p)
                if (k + 1) * JUMP <= half - w:
                    zcopy(w, (k + 1) * JUMP, p).start()
        for j in range(1, JUMP):
            for p in range(OUT):
                for w in range(2):
                    if k * JUMP + j <= half - w:
                        zcopy(w, k * JUMP + j, p).start()

    def landed(d, ways):
        for w in ways:
            bcopy(w, d).start()
        for w in ways:
            build(blk(-d if w == 0 else d))

    def crossed(d, ways):
        for w in ways:
            bwait(w, d)
            build(gz(-d if w == 0 else d) * 2 + 1 - c)

    def spread(lo, hi, what):
        def step(d, carry):
            what(d, (0, 1))
            return carry

        if lo < min(hi, half):
            lax.fori_loop(lo, min(hi, half), step, 0)
        if lo <= half < hi:
            what(half, (0,))

    def filled(d, ways):
        for p in range(OUT):
            for w in ways:
                zwait(w, d, p)
        landed(d, ways)

    def ring(stage, h):
        a = (pos1 if stage in (0, 3, 5) else pos2)[h]
        dev = (dev1 if stage in (0, 3, 5) else dev2)[h]
        nxt = [lax.rem(a + 1, 4), lax.rem(a + 3, 4)]
        return a, dev, nxt, lax.rem(a + 2, 4)

    def xcopy(stage, h, side, n, src, dst):
        _, dev, _, _ = ring(stage, h)
        return copy(src, dst, xsend.at[stage, h, side, n], xrecv.at[stage, h, side, n], dev[side])

    def rs_refs(stage, h):
        return (part[h], opp[h], main[h]) if stage == 0 else (s1[h], opp2[h], main2[h])

    def rs_copy(stage, h, side, n):
        _, _, nxt, far = ring(stage, h)
        src, o, m = rs_refs(stage, h)
        if n == 0:
            return xcopy(stage, h, side, 0, src.at[far, side], o.at[side])
        if n == 1:
            return xcopy(stage, h, side, 1, src.at[nxt[side], 1 - side], m.at[side, 1 - side])
        return xcopy(stage, h, side, 2, src.at[nxt[side], side], m.at[side, side])

    def rs_add(stage, h, side):
        _, _, nxt, _ = ring(stage, h)
        src, o, _ = rs_refs(stage, h)
        rs_copy(stage, h, side, 0).wait_recv()
        rows = src.shape[2]
        piece = min(rows, 128)

        def step(q, carry):
            at = pl.ds(pl.multiple_of(q * piece, piece), piece)
            total = src[nxt[side], side, at, :].astype(F32) + o[side, at, :].astype(F32)
            src[nxt[side], side, at, :] = total.astype(BF16)
            return carry

        lax.fori_loop(0, rows // piece, step, 0)
        rs_copy(stage, h, side, 2).start()

    def rs_wait_main(stage, h):
        for side in range(2):
            rs_copy(stage, h, side, 1).wait_recv()
            rs_copy(stage, h, side, 2).wait_recv()

    def ag_ref(stage, store, h, who, k):
        if stage in (3, 5):
            return store[h].at[who, k]
        a = pos1[h]
        return store[h].at[a, lax.div(who, 2), pl.ds(pl.multiple_of(lax.rem(who, 2) * hs + k * qs, qs), qs), :]

    def ag_copy(stage, store, h, side, n):
        a, _, nxt, _ = ring(stage, h)
        if n == 2:
            ref = ag_ref(stage, store, h, nxt[1 - side], side)
        else:
            ref = ag_ref(stage, store, h, a, side if n == 0 else 1 - side)
        return xcopy(stage, h, side, n, ref, ref)

    def ag_wait(stage, store, h, side, n):
        _, _, nxt, far = ring(stage, h)
        if n == 2:
            ref = ag_ref(stage, store, h, far, side)
        else:
            ref = ag_ref(stage, store, h, nxt[1 - side], side if n == 0 else 1 - side)
        xcopy(stage, h, side, n, ref, ref).wait_recv()

    def ag_send(stage, store, h):
        for n in range(2):
            for side in range(2):
                ag_copy(stage, store, h, side, n).start()

    def ag_pass(stage, store, h):
        for side in range(2):
            ag_wait(stage, store, h, side, 0)
            ag_copy(stage, store, h, side, 2).start()

    def ag_finish(stage, store, h):
        for side in range(2):
            ag_wait(stage, store, h, side, 1)
            ag_wait(stage, store, h, side, 2)

    def own_rows(h, k):
        return (pos1[h], lax.div(pos2[h], 2), pl.ds(pl.multiple_of(lax.rem(pos2[h], 2) * hs + k * qs, qs), qs))

    zpass(0)
    bcopy(0, 0).start()

    for h in range(2):
        for k in range(2):
            at = pl.ds(h * hs + k * qs, qs)
            v = gp_ref[at, :].astype(F32)
            a = v / (1.0 + jnp.exp(-v))
            act[at, :] = a
            i0, i1, i2 = own_rows(h, k)
            gh[h][i0, i1, i2, :] = (a * up_ref[at, :].astype(F32)).astype(BF16)
    for h in range(2):
        ag_send(2, gh, h)
    build(g)
    bwait(0, 0)
    build(z * 2 + 1 - c)

    def early(k):
        if k == 1:
            for h in range(2):
                ag_pass(2, gh, h)
        if k == 2:
            for h in range(2):
                ag_finish(2, gh, h)
                ag_send(3, gh, h)
        if k == 4:
            for h in range(2):
                ag_pass(3, gh, h)

    tops = half // JUMP
    for k in range(1, tops + 1):
        ways = (0, 1) if k * JUMP < half else (0,)
        zpass(k)
        landed(k * JUMP, ways)
        spread((k - 1) * JUMP + 1, k * JUMP, filled)
        early(k)
        if k > 1:
            spread((k - 2) * JUMP + 1, (k - 1) * JUMP + 1, crossed)
    spread(tops * JUMP + 1, half + 1, filled)
    for k in range(tops + 1, 5):
        early(k)
    spread((tops - 1) * JUMP + 1, half + 1, crossed)

    def partial(h, t):
        def step(q, carry):
            b = lax.div(q, 2)
            l = t * 4 + b if h == 0 else b * 4 + t
            rows = pl.ds(pl.multiple_of(h * hs + lax.rem(q, 2) * qs, qs), qs)
            v = jnp.dot(
                wbf[lax.div(l, per_e), rows, 0:feats],
                wd_ref[:, pl.ds(pl.multiple_of(l * hw, hw), hw)],
                preferred_element_type=F32,
            )
            part[h][t, lax.div(q, 4), pl.ds(pl.multiple_of(lax.rem(q, 4) * qs, qs), qs), :] = v.astype(BF16)
            return carry

        lax.fori_loop(0, 8, step, 0)

    for h in range(2):
        partial(h, ring(0, h)[3])
        for side in range(2):
            rs_copy(0, h, side, 0).start()
    for side in range(2):
        for h in range(2):
            partial(h, ring(0, h)[2][side])
            rs_copy(0, h, side, 1).start()
    for h in range(2):
        for side in range(2):
            rs_add(0, h, side)
    for h in range(2):
        partial(h, ring(0, h)[0])

    def turn(q, carry):
        at = pl.ds(pl.multiple_of(q * 128, 128), 128)
        for e in range(2):
            for k in range(0, wf.shape[2], 128):
                wt[e, k : k + 128, at] = wf[e, at, k : k + 128].T
        return carry

    lax.fori_loop(0, slots // 128, turn, 0)
    for e in range(2):
        top = jnp.max(jnp.abs(wt[e, 0:feats, :]), axis=1, keepdims=True) + 1e-6
        cst[e] = jnp.broadcast_to(top, (feats, 128))

    def scale(q, carry):
        at = pl.ds(pl.multiple_of(q * 128, 128), 128)
        for e in range(2):
            qt[e, :, at] = (wt[e, 0:feats, at] / cst[e]).astype(BF16)
        return carry

    lax.fori_loop(0, slots // 128, scale, 0)

    for h in range(2):
        rs_wait_main(0, h)

        def add1(q, carry):
            k = lax.div(q, 4)
            at = pl.ds(pl.multiple_of(lax.rem(q, 4) * qs, qs), qs)
            total = (
                part[h][pos1[h], k, at, :].astype(F32)
                + main[h][0, k, at, :].astype(F32)
                + main[h][1, k, at, :].astype(F32)
            )
            s1[h][lax.div(q, 2), lax.rem(q, 2)] = total.astype(BF16)
            return carry

        lax.fori_loop(0, 8, add1, 0)
        for side in range(2):
            rs_copy(1, h, side, 0).start()
            rs_copy(1, h, side, 1).start()
    for h in range(2):
        for side in range(2):
            rs_add(1, h, side)
    for h in range(2):
        ag_finish(3, gh, h)
    for h in range(2):
        rs_wait_main(1, h)
        for k in range(2):
            at = pl.ds(h * hs + k * qs, qs)
            total = (
                s1[h][pos2[h], k].astype(F32) + main2[h][0, k].astype(F32) + main2[h][1, k].astype(F32)
            )
            i0, i1, i2 = own_rows(h, k)
            gu[h][i0, i1, i2, :] = (total * act[at, :]).astype(BF16)
        ag_send(4, gu, h)
    for h in range(2):
        ag_pass(4, gu, h)
    for h in range(2):
        ag_finish(4, gu, h)
        ag_send(5, gu, h)

    def grad(q, carry):
        e = lax.div(q, per_e)
        xx, yy = lax.div(q, 4), lax.rem(q, 4)
        at = pl.ds(pl.multiple_of(q * hw, hw), hw)
        total = jnp.zeros((feats, hw), F32)
        for h, (i, j) in enumerate(((xx, yy), (yy, xx))):
            hid = gh[h][i, lax.div(j, 2), pl.ds(pl.multiple_of(lax.rem(j, 2) * hs, hs), hs), :]
            total += jnp.dot(qt[e, :, h * hs : (h + 1) * hs], hid, preferred_element_type=F32)
        dg_ref[:, at] = (total * cst[e]).astype(BF16)
        return carry

    lax.fori_loop(0, 8, grad, 0)
    for h in range(2):
        ag_pass(5, gu, h)
    lax.fori_loop(8, 16, grad, 0)
    for h in range(2):
        ag_finish(5, gu, h)

        def back(q, carry):
            total = jnp.zeros((qs, feats), F32)
            for i in range(4):
                for j in range(4):
                    l = i * 4 + j if h == 0 else j * 4 + i
                    up = gu[h][i, j // 2, pl.ds(pl.multiple_of((j % 2) * hs + q * qs, qs), qs), :]
                    total += lax.dot_general(up, wu_ref[:, l * hw : (l + 1) * hw], NT, preferred_element_type=F32)
            ret[pl.ds(pl.multiple_of(h * hs + q * qs, qs), qs), 0:feats] = total.astype(BF16)
            return carry

        lax.fori_loop(0, 2, back, 0)


    def contrib(n):
        zt = gz(n)
        i, j = zt * 2 + c, zt * 2 + 1 - c
        rows = jnp.concatenate(
            [
                ret[pl.ds(pl.multiple_of(i * cap, cap), cap), 0:feats],
                ret[pl.ds(pl.multiple_of(j * cap, cap), cap), 0:feats],
            ],
            axis=0,
        )
        mine, other = chosen(i)[0].astype(F32), chosen(j)[0].astype(F32)
        none = jnp.zeros((cap, toks), F32)
        pick = jnp.concatenate(
            [jnp.concatenate([mine, none], axis=1), jnp.concatenate([none, other], axis=1)], axis=0
        ).astype(BF16)
        v = lax.dot_general(rows, pick, TN, preferred_element_type=F32).astype(BF16)
        own[n] = v[:, 0:toks]
        sibs[n] = v[:, toks:]
        copy(sibs.at[n], sibr.at[n], csend.at[n], crecv.at[n], sib).start()

    def cwait(n):
        copy(sibs.at[n], sibr.at[n], csend.at[n], crecv.at[n], sib).wait_recv()

    def index(w, d):
        return d if w == 0 else lax.rem(n_z - d, n_z)

    rrows = feats // BACK

    def rcopy(w, d, p):
        b = base(d)
        dev = (blk(d - b if w == 0 else b - d), loc)
        at = pl.ds(p * rrows, rrows)
        return copy(
            rings.at[w, d - 1, at, :], ringr.at[w, d - 1, at, :], rsend.at[w, d - 1, p], rrecv.at[w, d - 1, p], dev
        )

    def here(n, p):
        at = pl.ds(p * rrows, rrows)
        return own[n, at, :].astype(F32) + sibr[n, at, :].astype(F32)

    def came(w, d, p):
        total = jnp.zeros((rrows, toks), F32)
        for j in range(1, JUMP + 1):
            if d + j <= half - w:
                rcopy(w, d + j, p).wait_recv()
                total += ringr[w, d + j - 1, pl.ds(p * rrows, rrows), :].astype(F32)
        return total

    def add(d, ways):
        for w in ways:
            contrib(index(w, d))

    def adds(k):
        if k == 0:
            contrib(0)
        spread(max(k * JUMP, 1), k * JUMP + JUMP if k < tops else half + 1, add)

    def leaf(d, ways):
        for w in ways:
            cwait(index(w, d))
        for p in range(BACK):
            for w in ways:
                rings[w, d - 1, pl.ds(p * rrows, rrows), :] = here(index(w, d), p).astype(BF16)
                rcopy(w, d, p).start()

    def leaves(k):
        spread(k * JUMP + 1, k * JUMP + JUMP if k < tops else half + 1, leaf)

    def lead(k):
        d = k * JUMP
        ways = (0, 1) if d < half else (0,)
        for w in ways:
            cwait(index(w, d))
        for p in range(BACK):
            for w in ways:
                total = here(index(w, d), p) + came(w, d, p)
                rings[w, d - 1, pl.ds(p * rrows, rrows), :] = total.astype(BF16)
                rcopy(w, d, p).start()

    for k in (tops, tops - 1):
        adds(k)
        leaves(k)
    for k in range(tops, 0, -1):
        if k > 1:
            adds(k - 2)
        lead(k)
        if k > 1:
            leaves(k - 2)
    cwait(0)
    for p in range(BACK):
        total = here(0, p) + came(0, 0, p) + came(1, 0, p)
        ig_ref[pl.ds(p * rrows, rrows), :] = total.astype(BF16)

    def drain(lo, hi, what):
        def step(s, carry):
            what(s)
            return carry
        lax.fori_loop(lo, hi, step, 0)

    for w in range(2):
        for p in range(OUT):
            drain(1, half + 1 - w, lambda d: zcopy(w, d, p).wait_send())
        for p in range(BACK):
            drain(1, half + 1 - w, lambda d: rcopy(w, d, p).wait_send())
    drain(0, half + 1, lambda s: bcopy(0, s).wait_send())
    drain(1, half, lambda s: bcopy(1, s).wait_send())
    drain(0, n_z, lambda n: copy(sibs.at[n], sibr.at[n], csend.at[n], crecv.at[n], sib).wait_send())
    for h in range(2):
        for side in range(2):
            for n in range(3):
                for stage in (0, 1):
                    rs_copy(stage, h, side, n).wait_send()
                for stage, store in ((2, gh), (3, gh), (4, gu), (5, gu)):
                    ag_copy(stage, store, h, side, n).wait_send()


def on_device(out_grad, group_choice, gate_weight, gate_pre, up_pre, down_weight, up_weight):
    n_grp = lax.axis_size("grp")
    half = n_grp // 4
    toks, feats = out_grad.shape
    picks, experts = gate_weight.shape[1:]
    slots, hw = gate_pre.shape[1:]
    hidden = down_weight.shape[1]
    hs, qs = slots // 2, slots // 4
    wide = -(-feats // 128) * 128
    vm = lambda shape, kind=BF16: pltpu.VMEM(shape, kind)
    sem = lambda *shape: pltpu.SemaphoreType.DMA(shape)
    meta = picks * (experts + 2)
    scratch = [
        vm((n_grp, feats + meta, toks)),
        vm((experts, slots, wide), F32), vm((experts, slots, wide)),
        vm((experts, wide, slots), F32), vm((experts, feats, slots)), vm((experts, feats, 128), F32),
        vm((slots, hw), F32),
        *[vm((4, 2, 2 * hs, hw)) for _ in range(6)],
        *[vm((2, 2 * hs, hw)) for _ in range(2)],
        *[vm((2, 2, 2 * hs, hw)) for _ in range(2)],
        *[vm((4, 2, qs, hw)) for _ in range(2)],
        *[vm((2, qs, hw)) for _ in range(2)],
        *[vm((2, 2, qs, hw)) for _ in range(2)],
        vm((slots, wide)),
        *[vm((n_grp // 2, feats, toks)) for _ in range(3)],
        *[vm((2, half, feats, toks)) for _ in range(2)],
        sem(2, half, OUT), sem(2, half, OUT), sem(2, half + 1), sem(2, half + 1),
        sem(6, 2, 2, 3), sem(6, 2, 2, 3),
        sem(2, half, BACK), sem(2, half, BACK), sem(n_grp // 2), sem(n_grp // 2),
    ]
    whole = pl.BlockSpec(memory_space=pltpu.VMEM)
    down_t, input_t = pl.pallas_call(
        moe_kernel,
        out_shape=(
            jax.ShapeDtypeStruct((feats, hidden), BF16),
            jax.ShapeDtypeStruct((feats, toks), BF16),
        ),
        in_specs=[whole] * 7,
        out_specs=(whole, whole),
        scratch_shapes=scratch,
        compiler_params=pltpu.CompilerParams(
            collective_id=0, has_side_effects=True, vmem_limit_bytes=58 * 1024 * 1024
        ),
    )(
        out_grad.T,
        group_choice.T,
        gate_weight.transpose(1, 2, 0).reshape(picks * experts, toks),
        gate_pre[0],
        up_pre[0],
        down_weight[0].T,
        up_weight[0].T,
    )
    return down_t.T[None], input_t.T


def solution(mesh):
    return jax.shard_map(
        on_device,
        mesh=mesh,
        in_specs=(
            P("grp", "loc"),
            P("grp", None),
            P("grp", None, None),
            P("grp", None, "loc"),
            P("grp", None, "loc"),
            P("grp", None, "loc"),
            P("grp", None, "loc"),
        ),
        out_specs=(P("grp", None, "loc"), P("grp", "loc")),
        check_vma=False,
    )
```
